256 devices in a mesh: expert: 128 (over y, x, z), row: 2 (over core).
Axes of the slice: x: 4, y: 4, z: 8, core: 2. Of those that a mesh axis runs over, the one named last changes fastest.
Arguments:
- calib_rows: bfloat16 [128, 128, 4096], P('expert', 'row'), may hold values from -6 to 6
- gate_weight: bfloat16 [128, 4096, 768], P('expert', 'row'), may hold values from -0.09375 to 0.09375
- up_weight: bfloat16 [128, 4096, 768], P('expert', 'row'), may hold values from -0.09375 to 0.09375
- cluster: int32 [128], replicated, may hold values from 0 to 31, never falling along the last dimension, each value on 1 to 8 neighbouring positions
- dominant_rank: int32 [32], replicated, may hold values from 0 to 7
Outputs:
- correlation: float32 [128, 768, 768], P('expert', 'row')
The draws below stay inside these ranges and needn't reach their ends.
Inputs may be any that keep to these rules, and one draw needn't show every extreme that they name: cluster numbers never fall along the expert index; each of the 32 clusters holds 1 to 8 experts, and one holds exactly 8.
All inputs are finite; a program needn't handle non-finite values.
Results may differ from the reference program's by a relative error of at most 0.0039.
Values may be sent and summed in bfloat16 or wider, within the bound.
No kernel may reach another device: no remote copies, remote signals or barrier semaphores. Data moves between devices by JAX's collectives and lax.ppermute only.
A program may use at most 256 MiB of HBM per device.

```python
import math
import jax
import jax.numpy as jnp
import numpy as np
from jax import lax

D = 4096
HID_WIN = 768
ROWS = 128
MAXC = 8
EXPERTS = 128
CLUSTERS = 32


def with_ends(entries, key, least, largest):
    extent = entries.shape
    spot = [jax.random.randint(jax.random.fold_in(key, axis), (), 0, extent[axis]) for axis in range(len(extent))]
    entries = entries.at[tuple(spot)].set(least)
    longest = extent.index(max(extent))
    spot[longest] = (spot[longest] + 1) % extent[longest]
    return entries.at[tuple(spot)].set(largest)


def block_levels(key, extent, pieces, least, top_value):
    def one(position, parts):
        draws = jax.random.uniform(jax.random.fold_in(jax.random.fold_in(key, 6), position), (parts,), jnp.float32, least / len(pieces), top_value / len(pieces))
        return jnp.repeat(jnp.exp(draws), extent[position] // parts).reshape((-1,) + (1,) * (len(extent) - position - 1))

    gain = one(*pieces[0])
    for cut in pieces[1:]:
        gain = gain * one(*cut)
    return gain


def profile(number_of, total, limit, slope):
    loads = [(1 << 20) // math.isqrt(standing ** slope) + 1 for standing in range(2, number_of + 1)]
    spare, given = total - limit - (number_of - 1), [1] * (number_of - 1)
    while spare > 0:
        candidates = [i for i in range(number_of - 1) if given[i] < limit]
        mass, remaining = sum([loads[i] for i in candidates]), spare
        for i in candidates:
            extra = min(limit - given[i], max(1, remaining * loads[i] // mass), spare)
            given[i] = given[i] + extra
            spare = spare - extra
    return np.array([limit] + given)


def uneven_parts(rng, number_of, total, bound, lean):
    if number_of == 2:
        one = jax.random.randint(rng, (), max(1, total - bound), min(bound, total - 1) + 1)
        return jnp.stack([one, total - one])
    tallies = jnp.asarray(profile(number_of, total, bound, lean), jnp.int32)
    pairs = (number_of - 1) // 2
    source_of, receiver = tallies[1:1 + 2 * pairs:2], tallies[2:2 + 2 * pairs:2]
    margin = jnp.minimum(source_of - 1, bound - receiver)
    passed = jax.random.randint(jax.random.fold_in(rng, 1), (pairs,), 0, 1 << 20) % (margin + 1)
    tallies = tallies.at[1:1 + 2 * pairs:2].set(source_of - passed).at[2:2 + 2 * pairs:2].set(receiver + passed)
    return tallies[jax.random.permutation(jax.random.fold_in(rng, 2), number_of)]


def scatter_about(rng, extent, spread, bound, shards=(), held_as=jnp.bfloat16):
    level = block_levels(rng, extent, shards, -0.22, 0.18) if shards else 1.0
    values = jax.random.normal(rng, extent, jnp.float32) * spread * level
    return jnp.minimum(jnp.maximum(values, -bound), bound).astype(held_as)


def setup_inputs(seed: int = 0) -> dict:
    splits = jax.random.split(jax.random.key(seed), 6)
    return {
        "calib_rows": scatter_about(splits[0], (EXPERTS, ROWS, D), 1.0, 6.0, ((0, 128), (1, 2))),
        "gate_weight": scatter_about(splits[1], (EXPERTS, D, HID_WIN), D ** -0.5, 0.09375, ((0, 128), (1, 2))),
        "up_weight": scatter_about(splits[2], (EXPERTS, D, HID_WIN), D ** -0.5, 0.09375, ((0, 128), (1, 2))),
        "cluster": jnp.searchsorted(jnp.cumsum(uneven_parts(splits[3], CLUSTERS, EXPERTS, MAXC, 2)), jnp.arange(EXPERTS), side="right").astype(jnp.int32),
        "dominant_rank": with_ends(jax.random.randint(splits[4], (CLUSTERS,), 0, MAXC), jax.random.fold_in(splits[4], 1), 0, MAXC - 1).astype(jnp.int32),
    }


def cluster_info(cluster, dominant_rank):
    start = lax.optimization_barrier(jnp.sum((cluster[None, :] < cluster[:, None]).astype(jnp.int32), axis=1)).astype(jnp.int32)
    size = lax.optimization_barrier(jnp.sum((cluster[None, :] == cluster[:, None]).astype(jnp.int32), axis=1)).astype(jnp.int32)
    ranks = dominant_rank[cluster]
    dom = (start + ranks % size).astype(jnp.int32)
    return (start, size, dom)

def reference(calib_rows, gate_weight, up_weight, cluster, dominant_rank):
    start, size, dom = cluster_info(cluster, dominant_rank)
    padding = jnp.zeros((MAXC, ROWS, D), calib_rows.dtype)
    padded = jnp.concatenate([calib_rows, padding], axis=0)

    def hidden_of(expert):
        union = lax.dynamic_slice_in_dim(padded, start[expert], MAXC, 0)
        keep = (jnp.arange(MAXC, dtype=jnp.int32) < size[expert])[:, None, None]
        union = jnp.where(keep, union, jnp.zeros_like(union)).reshape(MAXC * ROWS, D)
        gate = jnp.dot(union, gate_weight[expert], preferred_element_type=jnp.float32)
        up = jnp.dot(union, up_weight[expert], preferred_element_type=jnp.float32)
        return (jax.nn.silu(gate) * up).astype(jnp.bfloat16)
    hidden = lax.map(hidden_of, jnp.arange(EXPERTS, dtype=jnp.int32))

    def correlate(expert):
        sums = jnp.dot(hidden[expert].T, hidden[dom[expert]], preferred_element_type=jnp.float32)
        return sums / jnp.sqrt((size[expert] * ROWS).astype(jnp.float32))
    return lax.map(correlate, jnp.arange(EXPERTS, dtype=jnp.int32))
```

```python
import jax
import jax.numpy as jnp
from jax import lax
from jax.sharding import PartitionSpec as P

ROWS = 128
LINE = 8
OFFSETS = (1, 7, 2, 6, 3, 5, 4)
PAIRS = ((1, 7), (2, 6), (3, 5), (4,))


def along_line(value, offset):
    count = lax.axis_size("expert")
    pairs = [(i, i // LINE * LINE + (i - offset) % LINE) for i in range(count)]
    return lax.ppermute(value, "expert", pairs)


def to_line(value, step):
    count = lax.axis_size("expert")
    return lax.ppermute(value, "expert", [(i, (i + step * LINE) % count) for i in range(count)])


def to_side(value, offset):
    count = lax.axis_size("expert")
    side = lambda i: LINE if i % LINE + offset < LINE else -LINE
    return lax.ppermute(value, "expert", [(i, (i + side(i)) % count) for i in range(count)])


def swap_cores(value):
    return lax.ppermute(value, "row", [(0, 1), (1, 0)])


def neighbourhood(table, line, place):
    fill = jnp.full((LINE,), -1, table.dtype)
    three = lax.dynamic_slice_in_dim(jnp.concatenate([fill, table, fill]), line * LINE, 3 * LINE).reshape(3, LINE)
    return lax.dynamic_slice_in_dim(jnp.concatenate([three, three], axis=1), place, LINE, 1)


def per_device(calib_rows, gate_weight, up_weight, cluster, dominant_rank):
    expert_id = lax.axis_index("expert")
    core = lax.axis_index("row")
    line, place = expert_id // LINE, expert_id % LINE

    start = jnp.sum((cluster[None, :] < cluster[:, None]).astype(jnp.int32), axis=1)
    size = jnp.sum((cluster[None, :] == cluster[:, None]).astype(jnp.int32), axis=1)
    names = jnp.arange(dominant_rank.shape[0], dtype=jnp.int32)
    rank = jnp.sum(jnp.where(names[None, :] == cluster[:, None], dominant_rank[None, :], 0), axis=1)
    dom = start + rank % size
    near = neighbourhood(cluster, line, place)
    near_dom = neighbourhood(dom, line, place)
    mine, my_dom = near[1, 0], near_dom[1, 0]
    my_size = jnp.sum((cluster == mine).astype(jnp.int32))
    valid = jnp.any(near == mine, axis=0)
    wants_last = near[1] == near[0, 0]
    wants_next = near[1] == near[2, 0]
    ends = jnp.pad(cluster, (LINE, LINE), constant_values=-1)
    to_last = ends[line * LINE + LINE - 1] == mine
    to_next = ends[line * LINE + 2 * LINE] == mine

    gate_own, up_own = gate_weight[0], up_weight[0]
    gate_other, up_other = swap_cores(gate_own), swap_cores(up_own)
    half = gate_own.shape[0]

    def hidden_of(rows):
        mine_part = lax.dynamic_slice_in_dim(rows, core * half, half, 1)
        other_part = lax.dynamic_slice_in_dim(rows, (1 - core) * half, half, 1)
        dot = lambda a, b: jnp.dot(a, b, preferred_element_type=jnp.float32)
        gate = dot(mine_part, gate_own) + dot(other_part, gate_other)
        up = dot(mine_part, up_own) + dot(other_part, up_other)
        return (jax.nn.silu(gate) * up).astype(jnp.bfloat16)

    def for_receiver(offset, own, last, nxt):
        away = (-offset) % LINE
        return jnp.where(wants_last[away], last, jnp.where(wants_next[away], nxt, own))

    own = calib_rows[0]
    part = own.shape[0]
    ring, beside = {0: own}, {}
    for step in range(1, LINE // 2 + 1):
        ring[step] = along_line(ring[step - 1], 1)
        if step < LINE // 2:
            ring[LINE - step] = along_line(ring[(LINE - step + 1) % LINE], -1)
    for k in ring:
        if k:
            beside[k] = to_side(ring[k], k)
    arrived = {k: jnp.where(near[1, k] == mine, ring[k], beside[k]) for k in beside}

    hidden = {0: hidden_of(own)}
    for pair in PAIRS:
        block = hidden_of(jnp.concatenate([arrived[k] for k in pair], axis=0))
        for n, k in enumerate(pair):
            hidden[k] = jnp.where(valid[k], block[n * part : (n + 1) * part], jnp.zeros((), jnp.bfloat16))
    returned = {0: hidden[0]}
    for k in OFFSETS:
        returned[LINE - k] = along_line(hidden[k], LINE - k)

    def from_dom(target):
        value = returned[0]
        for k in OFFSETS:
            value = jnp.where(line * LINE + (place + k) % LINE == target, returned[k], value)
        return value

    share_own = from_dom(my_dom)
    share_next = from_dom(jnp.where(to_next, my_dom, near_dom[2, 0]))
    share_last = from_dom(jnp.where(to_last, my_dom, near_dom[0, 0]))
    came_last, came_next = to_line(share_next, 1), to_line(share_last, -1)
    chunk_own = jnp.where(
        my_dom // LINE == line, share_own, jnp.where(my_dom // LINE > line, came_next, came_last)
    )
    chunk_last = jnp.where(near_dom[0, 0] // LINE == line, share_last, came_last)
    chunk_next = jnp.where(near_dom[2, 0] // LINE == line, share_next, came_next)
    panel = {0: chunk_own}
    for k in OFFSETS:
        panel[k] = along_line(for_receiver(k, chunk_own, chunk_last, chunk_next), k)

    order = (0,) + OFFSETS
    shares = lax.dot_general(
        jnp.concatenate([hidden[k] for k in order], axis=0),
        jnp.concatenate([panel[k] for k in order], axis=0),
        (((0,), (0,)), ((), ())),
        preferred_element_type=jnp.float32,
    )
    rows_out = shares.shape[0] // 2
    keep = lax.dynamic_slice_in_dim(shares, core * rows_out, rows_out, 0)
    give = lax.dynamic_slice_in_dim(shares, (1 - core) * rows_out, rows_out, 0)
    total = keep + swap_cores(give)
    return (total / jnp.sqrt((my_size * ROWS).astype(jnp.float32)))[None]


def solution(mesh):
    return jax.shard_map(
        per_device,
        mesh=mesh,
        in_specs=(
            P("expert", "row", None),
            P("expert", "row", None),
            P("expert", "row", None),
            P(),
            P(),
        ),
        out_specs=P("expert", "row", None),
        check_vma=False,
    )
```

```python
import functools

import jax
import jax.numpy as jnp
from jax import lax
from jax.experimental import pallas as pl
from jax.experimental.pallas import tpu as pltpu
from jax.sharding import PartitionSpec as P

ROWS = 128
LINE = 8
TILE = 512
OFFSETS = (1, 7, 2, 6, 3, 5, 4)
GROUPS = ((0, 1, 7), (2, 6), (3, 5), (4,))

NEAR, DOM, CORE, LINE_AT, PLACE, SIZE = 0, 24, 48, 49, 50, 51


def along_line(value, offset):
    count = lax.axis_size("expert")
    pairs = [(i, i // LINE * LINE + (i - offset) % LINE) for i in range(count)]
    return lax.ppermute(value, "expert", pairs)


def to_line(value, step):
    count = lax.axis_size("expert")
    return lax.ppermute(value, "expert", [(i, (i + step * LINE) % count) for i in range(count)])


def to_side(value, offset):
    count = lax.axis_size("expert")
    side = lambda i: LINE if i % LINE + offset < LINE else -LINE
    return lax.ppermute(value, "expert", [(i, (i + side(i)) % count) for i in range(count)])


def swap_cores(value):
    return lax.ppermute(value, "row", [(0, 1), (1, 0)])


def scalars(cluster, dominant_rank):
    expert_id = lax.axis_index("expert")
    line, place = expert_id // LINE, expert_id % LINE
    start = jnp.sum((cluster[None, :] < cluster[:, None]).astype(jnp.int32), axis=1)
    size = jnp.sum((cluster[None, :] == cluster[:, None]).astype(jnp.int32), axis=1)
    names = jnp.arange(dominant_rank.shape[0], dtype=jnp.int32)
    rank = jnp.sum(jnp.where(names[None, :] == cluster[:, None], dominant_rank[None, :], 0), axis=1)
    dom = start + rank % size
    tables = jnp.pad(jnp.stack([cluster, dom, size]), ((0, 0), (LINE, LINE)), constant_values=-1)
    three = lax.dynamic_slice_in_dim(tables, line * LINE, 3 * LINE, 1).reshape(3, 3, LINE)
    rolled = lax.dynamic_slice_in_dim(jnp.concatenate([three, three], axis=2), place, LINE, 2)
    here = jnp.stack([lax.axis_index("row"), line, place, rolled[2, 1, 0]])
    return jnp.concatenate([rolled[:2].reshape(-1), here]).astype(jnp.int32)


def near(table, line, k):
    return table[NEAR + LINE * line + k]


def hidden_kernel(group, table, *refs):
    many = len(group)
    xs, weights = refs[: 4 * many], refs[4 * many : 4 * many + 4]
    outs, (gate_sum, up_sum) = refs[4 * many + 4 : 5 * many + 4], refs[5 * many + 4 :]
    step = pl.program_id(0)
    mine = near(table, 1, 0)

    @pl.when(step == 0)
    def _():
        gate_sum[...] = jnp.zeros_like(gate_sum)
        up_sum[...] = jnp.zeros_like(up_sum)

    for side in range(2):
        rows = []
        for n, k in enumerate(group):
            ring, beside = xs[4 * n + side], xs[4 * n + 2 + side]
            rows.append(ring[...] if k == 0 else jnp.where(near(table, 1, k) == mine, ring[...], beside[...]))
        rows = jnp.concatenate(rows, axis=0)
        gate_sum[...] += jnp.dot(rows, weights[side][...], preferred_element_type=jnp.float32)
        up_sum[...] += jnp.dot(rows, weights[2 + side][...], preferred_element_type=jnp.float32)

    @pl.when(step == pl.num_programs(0) - 1)
    def _():
        gate = gate_sum[...]
        value = gate / (1.0 + jnp.exp(-gate)) * up_sum[...]
        part = outs[0].shape[0]
        for n, k in enumerate(group):
            block = value[n * part : (n + 1) * part].astype(jnp.bfloat16)
            inside = (near(table, 0, k) == mine) | (near(table, 1, k) == mine) | (near(table, 2, k) == mine)
            outs[n][...] = jnp.where(inside, block, jnp.zeros_like(block))


def hidden_of(table, group, ring, beside, weights):
    part, width = ring[0].shape
    half, units = weights[0].shape
    steps = half // TILE
    own_half = pl.BlockSpec((part, TILE), lambda i, t: (0, t[CORE] * steps + i))
    other_half = pl.BlockSpec((part, TILE), lambda i, t: (0, (1 - t[CORE]) * steps + i))
    weight = pl.BlockSpec((TILE, units), lambda i, t: (i, 0))
    args, specs = [], []
    for k in group:
        args += [ring[k], ring[k], beside.get(k, ring[k]), beside.get(k, ring[k])]
        specs += [own_half, other_half, own_half, other_half]
    rows = part * len(group)
    return pl.pallas_call(
        functools.partial(hidden_kernel, group),
        out_shape=[jax.ShapeDtypeStruct((part, units), jnp.bfloat16)] * len(group),
        grid_spec=pltpu.PrefetchScalarGridSpec(
            num_scalar_prefetch=1,
            grid=(steps,),
            in_specs=specs + [weight] * 4,
            out_specs=[pl.BlockSpec((part, units), lambda i, t: (0, 0))] * len(group),
            scratch_shapes=[pltpu.VMEM((rows, units), jnp.float32)] * 2,
        ),
        compiler_params=pltpu.CompilerParams(vmem_limit_bytes=40 << 20),
        cost_estimate=pl.CostEstimate(
            flops=4 * rows * width * units, bytes_accessed=8 * half * units + 4 * rows * width, transcendentals=rows * units
        ),
        name="hidden",
    )(table, *args, *weights)


def goes_on(table, to):
    edge = (LINE - 1 - table[PLACE]) if to == 0 else (LINE - table[PLACE]) % LINE
    return near(table, to, edge) == near(table, 1, 0)


def dom_of(table, line):
    return table[DOM + LINE * line]


def share_kernel(table, *refs):
    returned, outs = refs[:LINE], refs[LINE:]
    own = dom_of(table, 1)
    targets = (own, jnp.where(goes_on(table, 2), own, dom_of(table, 2)), jnp.where(goes_on(table, 0), own, dom_of(table, 0)))
    for out, target in zip(outs, targets):
        place = (target - table[PLACE]) & (LINE - 1)
        for k in range(LINE):

            @pl.when(place == k)
            def _():
                out[...] = returned[k][...]


def send_kernel(table, own, nxt, last, came_last, came_next, *outs):
    line = table[LINE_AT]
    dom = [lax.div(dom_of(table, n) + LINE, LINE) - 1 for n in range(3)]
    at_own = jnp.where(dom[1] == line, 0, jnp.where(dom[1] > line, 4, 3))
    at_last = jnp.where(dom[0] == line, 2, 3)
    at_next = jnp.where(dom[2] == line, 1, 4)
    sources = (own, nxt, last, came_last, came_next)
    for away in range(LINE):
        wanted = near(table, 1, away)
        source = jnp.where(wanted == near(table, 0, 0), at_last, jnp.where(wanted == near(table, 2, 0), at_next, at_own))
        for n, ref in enumerate(sources):

            @pl.when(source == n)
            def _():
                outs[away][...] = ref[...]


def choose(kernel, table, arrays, outs, name):
    whole = pl.BlockSpec(memory_space=pltpu.VMEM)
    shape = jax.ShapeDtypeStruct(arrays[0].shape, arrays[0].dtype)
    size = 2 * arrays[0].size
    return pl.pallas_call(
        kernel,
        out_shape=[shape] * outs,
        in_specs=[pl.BlockSpec(memory_space=pltpu.SMEM)] + [whole] * len(arrays),
        out_specs=[whole] * outs,
        compiler_params=pltpu.CompilerParams(vmem_limit_bytes=24 << 20),
        cost_estimate=pl.CostEstimate(flops=0, bytes_accessed=size * (len(arrays) + outs), transcendentals=0),
        name=name,
    )(table, *arrays)


def correlate_kernel(add, table, *refs):
    hidden, panel = refs[:LINE], refs[LINE : 2 * LINE]
    out = refs[-1]
    left = jnp.concatenate([ref[...] for ref in hidden], axis=0)
    right = jnp.concatenate([ref[...] for ref in panel], axis=0)
    sums = lax.dot_general(left, right, (((0,), (0,)), ((), ())), preferred_element_type=jnp.float32)
    if add:
        rows = jnp.full((1, 1), table[SIZE] * ROWS, jnp.int32).astype(jnp.float32)
        sums = (sums + refs[2 * LINE][...]) / jnp.sqrt(rows)
    out[...] = sums


def correlate(table, hidden, panel, received=None):
    part, units = hidden[0].shape
    add = received is not None
    core = (lambda t: t[CORE]) if add else (lambda t: 1 - t[CORE])
    tile = 128
    steps = units // 2 // tile
    left = pl.BlockSpec((part, tile), lambda i, t: (0, core(t) * steps + i))
    right = pl.BlockSpec((part, units), lambda i, t: (0, 0))
    result = pl.BlockSpec((tile, units), lambda i, t: (i, 0))
    extra = [received] if add else []
    return pl.pallas_call(
        functools.partial(correlate_kernel, add),
        out_shape=jax.ShapeDtypeStruct((units // 2, units), jnp.float32),
        grid_spec=pltpu.PrefetchScalarGridSpec(
            num_scalar_prefetch=1,
            grid=(steps,),
            in_specs=[left] * LINE + [right] * LINE + [result] * len(extra),
            out_specs=result,
        ),
        compiler_params=pltpu.CompilerParams(vmem_limit_bytes=24 << 20),
        cost_estimate=pl.CostEstimate(
            flops=LINE * part * units * units, bytes_accessed=32 * part * units, transcendentals=0
        ),
        name="correlate",
    )(table, *hidden, *panel, *extra)


def per_device(calib_rows, gate_weight, up_weight, cluster, dominant_rank):
    table = scalars(cluster, dominant_rank)

    ring, beside = {0: calib_rows[0]}, {}
    for step in range(1, LINE // 2 + 1):
        ring[step] = along_line(ring[step - 1], 1)
        if step < LINE // 2:
            ring[LINE - step] = along_line(ring[(LINE - step + 1) % LINE], -1)
    gate, up = gate_weight[0], up_weight[0]
    weights = (gate, swap_cores(gate), up, swap_cores(up))

    hidden, returned = {}, {}
    for group in GROUPS:
        for k in group:
            if k:
                beside[k] = to_side(ring[k], k)
        for k, block in zip(group, hidden_of(table, group, ring, beside, weights)):
            hidden[k] = block
            returned[(LINE - k) % LINE] = along_line(block, LINE - k) if k else block

    shares = choose(share_kernel, table, [returned[k] for k in range(LINE)], 3, "share")
    came_last, came_next = to_line(shares[1], 1), to_line(shares[2], -1)
    chunks = choose(send_kernel, table, [*shares, came_last, came_next], LINE, "send")
    panel = {k: along_line(chunks[(-k) % LINE], k) if k else chunks[0] for k in range(LINE)}

    hidden, panel = [hidden[k] for k in range(LINE)], [panel[k] for k in range(LINE)]
    received = swap_cores(correlate(table, hidden, panel))
    return correlate(table, hidden, panel, received)[None]


def solution(mesh):
    return jax.shard_map(
        per_device,
        mesh=mesh,
        in_specs=(
            P("expert", "row", None),
            P("expert", "row", None),
            P("expert", "row", None),
            P(),
            P(),
        ),
        out_specs=P("expert", "row", None),
        check_vma=False,
    )
```

```python
import functools

import jax
import jax.numpy as jnp
from jax import lax
from jax.experimental import pallas as pl
from jax.experimental.pallas import tpu as pltpu
from jax.sharding import PartitionSpec as P

ROWS = 128
LINE = 8
TILE = 512

NEAR, DOM, CORE, LINE_AT, PLACE, SIZE = 0, 24, 48, 49, 50, 51


def along_line(value, offset):
    count = lax.axis_size("expert")
    pairs = [(i, i // LINE * LINE + (i - offset) % LINE) for i in range(count)]
    return lax.ppermute(value, "expert", pairs)


def shift(value, step):
    count = lax.axis_size("expert")
    return lax.ppermute(value, "expert", [(i, (i + step) % count) for i in range(count)])


def swap_cores(value):
    return lax.ppermute(value, "row", [(0, 1), (1, 0)])


def after(*values):
    return lax.optimization_barrier(values)


def scalars(cluster, dominant_rank):
    expert_id = lax.axis_index("expert")
    line, place = expert_id // LINE, expert_id % LINE
    start = jnp.sum((cluster[None, :] < cluster[:, None]).astype(jnp.int32), axis=1)
    size = jnp.sum((cluster[None, :] == cluster[:, None]).astype(jnp.int32), axis=1)
    names = jnp.arange(dominant_rank.shape[0], dtype=jnp.int32)
    rank = jnp.sum(jnp.where(names[None, :] == cluster[:, None], dominant_rank[None, :], 0), axis=1)
    dom = start + rank % size
    tables = jnp.pad(jnp.stack([cluster, dom, size]), ((0, 0), (LINE, LINE)), constant_values=-1)
    three = lax.dynamic_slice_in_dim(tables, line * LINE, 3 * LINE, 1).reshape(3, 3, LINE)
    rolled = lax.dynamic_slice_in_dim(jnp.concatenate([three, three], axis=2), place, LINE, 2)
    here = jnp.stack([lax.axis_index("row"), line, place, rolled[2, 1, 0]])
    return jnp.concatenate([rolled[:2].reshape(-1), here]).astype(jnp.int32)


def near(table, line, k):
    return table[NEAR + LINE * line + k]


def cluster_at(table, k):
    if k >= 0:
        return jnp.where(table[PLACE] + k < LINE, near(table, 1, k), near(table, 2, k))
    return jnp.where(table[PLACE] + k >= 0, near(table, 1, k + LINE), near(table, 0, k + LINE))


def hidden_kernel(group, table, *refs):
    many = len(group)
    xs, weights = refs[: 4 * many], refs[4 * many : 4 * many + 4]
    outs, (gate_sum, up_sum) = refs[4 * many + 4 : 5 * many + 4], refs[5 * many + 4 :]
    step = pl.program_id(0)
    mine = near(table, 1, 0)

    @pl.when(step == 0)
    def _():
        gate_sum[...] = jnp.zeros_like(gate_sum)
        up_sum[...] = jnp.zeros_like(up_sum)

    for side in range(2):
        rows = []
        for n, k in enumerate(group):
            ahead, behind = xs[4 * n + side], xs[4 * n + 2 + side]
            rows.append(ahead[...] if k == 0 else jnp.where(cluster_at(table, k) == mine, ahead[...], behind[...]))
        rows = jnp.concatenate(rows, axis=0)
        gate_sum[...] += jnp.dot(rows, weights[side][...], preferred_element_type=jnp.float32)
        up_sum[...] += jnp.dot(rows, weights[2 + side][...], preferred_element_type=jnp.float32)

    @pl.when(step == pl.num_programs(0) - 1)
    def _():
        gate = gate_sum[...]
        value = gate / (1.0 + jnp.exp(-gate)) * up_sum[...]
        part = outs[0].shape[0]
        for n, k in enumerate(group):
            block = value[n * part : (n + 1) * part].astype(jnp.bfloat16)
            inside = (cluster_at(table, k) == mine) | (cluster_at(table, k - LINE if k else 0) == mine)
            outs[n][...] = jnp.where(inside, block, jnp.zeros_like(block))


def hidden_of(table, group, ahead, behind, weights):
    part, width = ahead[0].shape
    half, units = weights[0].shape
    steps = half // TILE
    own_half = pl.BlockSpec((part, TILE), lambda i, t: (0, t[CORE] * steps + i))
    other_half = pl.BlockSpec((part, TILE), lambda i, t: (0, (1 - t[CORE]) * steps + i))
    weight = pl.BlockSpec((TILE, units), lambda i, t: (i, 0))
    args, specs = [], []
    for k in group:
        args += [ahead[k], ahead[k], behind[k], behind[k]]
        specs += [own_half, other_half, own_half, other_half]
    rows = part * len(group)
    return pl.pallas_call(
        functools.partial(hidden_kernel, group),
        out_shape=[jax.ShapeDtypeStruct((part, units), jnp.bfloat16)] * len(group),
        grid_spec=pltpu.PrefetchScalarGridSpec(
            num_scalar_prefetch=1,
            grid=(steps,),
            in_specs=specs + [weight] * 4,
            out_specs=[pl.BlockSpec((part, units), lambda i, t: (0, 0))] * len(group),
            scratch_shapes=[pltpu.VMEM((rows, units), jnp.float32)] * 2,
        ),
        compiler_params=pltpu.CompilerParams(vmem_limit_bytes=40 << 20),
        cost_estimate=pl.CostEstimate(
            flops=4 * rows * width * units, bytes_accessed=8 * half * units + 4 * rows * width, transcendentals=rows * units
        ),
        name="hidden",
    )(table, *args, *weights)


def goes_on(table, to):
    edge = (LINE - 1 - table[PLACE]) if to == 0 else (LINE - table[PLACE]) % LINE
    return near(table, to, edge) == near(table, 1, 0)


def dom_of(table, line):
    return table[DOM + LINE * line]


def share_kernel(table, *refs):
    returned, outs = refs[:LINE], refs[LINE:]
    own = dom_of(table, 1)
    targets = (own, jnp.where(goes_on(table, 2), own, dom_of(table, 2)), jnp.where(goes_on(table, 0), own, dom_of(table, 0)))
    for out, target in zip(outs, targets):
        place = (target - table[PLACE]) & (LINE - 1)
        for k in range(LINE):

            @pl.when(place == k)
            def _():
                out[...] = returned[k][...]


def send_kernel(table, own, nxt, last, came_last, came_next, *outs):
    line = table[LINE_AT]
    dom = [lax.div(dom_of(table, n) + LINE, LINE) - 1 for n in range(3)]
    at_own = jnp.where(dom[1] == line, 0, jnp.where(dom[1] > line, 4, 3))
    at_last = jnp.where(dom[0] == line, 2, 3)
    at_next = jnp.where(dom[2] == line, 1, 4)
    sources = (own, nxt, last, came_last, came_next)
    for away in range(LINE):
        wanted = near(table, 1, away)
        source = jnp.where(wanted == near(table, 0, 0), at_last, jnp.where(wanted == near(table, 2, 0), at_next, at_own))
        for n, ref in enumerate(sources):

            @pl.when(source == n)
            def _():
                outs[away][...] = ref[...]


def forward_kernel(table, back_three, ahead_six, ahead_three, back_six, to_next, to_last):
    def pick(out, far, near_by, receiver):
        wants_far = cluster_at(table, 6 * receiver) == cluster_at(table, receiver)

        @pl.when(wants_far)
        def _():
            out[...] = far[...]

        @pl.when(jnp.logical_not(wants_far))
        def _():
            out[...] = near_by[...]

    pick(to_next, ahead_six, back_three, 1)
    pick(to_last, back_six, ahead_three, -1)


def choose(kernel, table, arrays, outs, name):
    whole = pl.BlockSpec(memory_space=pltpu.VMEM)
    shape = jax.ShapeDtypeStruct(arrays[0].shape, arrays[0].dtype)
    size = 2 * arrays[0].size
    return pl.pallas_call(
        kernel,
        out_shape=[shape] * outs,
        in_specs=[pl.BlockSpec(memory_space=pltpu.SMEM)] + [whole] * len(arrays),
        out_specs=[whole] * outs,
        compiler_params=pltpu.CompilerParams(vmem_limit_bytes=24 << 20),
        cost_estimate=pl.CostEstimate(flops=0, bytes_accessed=size * (len(arrays) + outs), transcendentals=0),
        name=name,
    )(table, *arrays)


def correlate_kernel(add, table, *refs):
    hidden, panel = refs[:LINE], refs[LINE : 2 * LINE]
    out = refs[-1]
    left = jnp.concatenate([ref[...] for ref in hidden], axis=0)
    right = jnp.concatenate([ref[...] for ref in panel], axis=0)
    sums = lax.dot_general(left, right, (((0,), (0,)), ((), ())), preferred_element_type=jnp.float32)
    if add:
        rows = jnp.full((1, 1), table[SIZE] * ROWS, jnp.int32).astype(jnp.float32)
        sums = (sums + refs[2 * LINE][...]) / jnp.sqrt(rows)
    out[...] = sums


def correlate(table, hidden, panel, received=None):
    part, units = hidden[0].shape
    add = received is not None
    core = (lambda t: t[CORE]) if add else (lambda t: 1 - t[CORE])
    tile = 128
    steps = units // 2 // tile
    left = pl.BlockSpec((part, tile), lambda i, t: (0, core(t) * steps + i))
    right = pl.BlockSpec((part, units), lambda i, t: (0, 0))
    result = pl.BlockSpec((tile, units), lambda i, t: (i, 0))
    extra = [received] if add else []
    return pl.pallas_call(
        functools.partial(correlate_kernel, add),
        out_shape=jax.ShapeDtypeStruct((units // 2, units), jnp.float32),
        grid_spec=pltpu.PrefetchScalarGridSpec(
            num_scalar_prefetch=1,
            grid=(steps,),
            in_specs=[left] * LINE + [right] * LINE + [result] * len(extra),
            out_specs=result,
        ),
        compiler_params=pltpu.CompilerParams(vmem_limit_bytes=24 << 20),
        cost_estimate=pl.CostEstimate(
            flops=LINE * part * units * units, bytes_accessed=32 * part * units, transcendentals=0
        ),
        name="correlate",
    )(table, *hidden, *panel, *extra)


def per_device(calib_rows, gate_weight, up_weight, cluster, dominant_rank):
    table = scalars(cluster, dominant_rank)

    gate, up = gate_weight[0], up_weight[0]
    gate_other, up_other = swap_cores(gate), swap_cores(up)
    own = calib_rows[0]
    ahead, behind = {0: own}, {0: own}
    ahead[1], behind[7] = shift(own, -1), shift(own, 1)
    ahead[1], behind[7], gate_other, up_other = after(ahead[1], behind[7], gate_other, up_other)
    weights = (gate, gate_other, up, up_other)
    ahead[2], behind[6] = shift(ahead[1], -1), shift(behind[7], 1)
    behind[1], ahead[7] = shift(ahead[1], LINE), shift(behind[7], -LINE)
    ahead[2], behind[6], behind[1], ahead[7] = after(ahead[2], behind[6], behind[1], ahead[7])
    ahead[3], behind[5] = shift(ahead[2], -1), shift(behind[6], 1)
    behind[2], ahead[6] = shift(ahead[2], LINE), shift(behind[6], -LINE)

    hidden, returned = {}, {}

    def compute(group):
        for k, block in zip(group, hidden_of(table, group, ahead, behind, weights)):
            hidden[k] = block
            returned[(LINE - k) % LINE] = along_line(block, LINE - k) if k else block

    compute((0, 1, 7))
    ahead[3], behind[5], ahead[6], behind[2], hidden[0] = after(ahead[3], behind[5], ahead[6], behind[2], hidden[0])
    to_next, to_last = choose(forward_kernel, table, [behind[5], ahead[6], ahead[3], behind[2]], 2, "forward")
    from_last, from_next = shift(to_next, 1), shift(to_last, -1)
    ahead[4], behind[3], behind[4], ahead[5] = from_next, from_next, from_last, from_last
    compute((2, 6))
    compute((3, 5, 4))

    shares = choose(share_kernel, table, [returned[k] for k in range(LINE)], 3, "share")
    came_last, came_next = shift(shares[1], LINE), shift(shares[2], -LINE)
    chunks = choose(send_kernel, table, [*shares, came_last, came_next], LINE, "send")
    panel = {k: along_line(chunks[(-k) % LINE], k) if k else chunks[0] for k in range(LINE)}

    hidden, panel = [hidden[k] for k in range(LINE)], [panel[k] for k in range(LINE)]
    received = swap_cores(correlate(table, hidden, panel))
    return correlate(table, hidden, panel, received)[None]


def solution(mesh):
    return jax.shard_map(
        per_device,
        mesh=mesh,
        in_specs=(
            P("expert", "row", None),
            P("expert", "row", None),
            P("expert", "row", None),
            P(),
            P(),
        ),
        out_specs=P("expert", "row", None),
        check_vma=False,
    )
```

```python
import functools

import jax
import jax.numpy as jnp
from jax import lax
from jax.experimental import pallas as pl
from jax.experimental.pallas import tpu as pltpu
from jax.sharding import PartitionSpec as P

ROWS = 128
LINE = 8
TILE = 512

NEAR, DOM, CORE, LINE_AT, PLACE, SIZE = 0, 24, 48, 49, 50, 51


def moved(value, target):
    count = lax.axis_size("expert")
    return lax.ppermute(value, "expert", [(i, target(i) % count) for i in range(count)])


def with_next(value):
    return moved(value, lambda i: i + 1 - 2 * (i % 2))


def with_last(value):
    return moved(value, lambda i: i - 1 + 2 * (i % 2))


def to_line(value, step):
    return moved(value, lambda i: i + step * LINE * (1 - 2 * (i % 2)))


def round_line(value, offset):
    turn = lambda i: i // LINE * LINE + (i + offset * (1 - 2 * (i % 2))) % LINE
    return moved(value, turn), (offset if offset % 2 else LINE - offset)


def swap_cores(value):
    return lax.ppermute(value, "row", [(0, 1), (1, 0)])


def after(*values):
    return lax.optimization_barrier(values)


def scalars(cluster, dominant_rank):
    expert_id = lax.axis_index("expert")
    top = cluster.shape[0] - 1
    mirrored = expert_id % 2 == 1
    expert_id = jnp.where(mirrored, top - expert_id, expert_id)
    line, place = expert_id // LINE, expert_id % LINE
    start = jnp.sum((cluster[None, :] < cluster[:, None]).astype(jnp.int32), axis=1)
    size = jnp.sum((cluster[None, :] == cluster[:, None]).astype(jnp.int32), axis=1)
    names = jnp.arange(dominant_rank.shape[0], dtype=jnp.int32)
    rank = jnp.sum(jnp.where(names[None, :] == cluster[:, None], dominant_rank[None, :], 0), axis=1)
    dom = start + rank % size
    tables = jnp.where(mirrored, jnp.stack([cluster, top - dom, size])[:, ::-1], jnp.stack([cluster, dom, size]))
    tables = jnp.pad(tables, ((0, 0), (LINE, LINE)), constant_values=-1)
    three = lax.dynamic_slice_in_dim(tables, line * LINE, 3 * LINE, 1).reshape(3, 3, LINE)
    rolled = lax.dynamic_slice_in_dim(jnp.concatenate([three, three], axis=2), place, LINE, 2)
    here = jnp.stack([lax.axis_index("row"), line, place, rolled[2, 1, 0]])
    return jnp.concatenate([rolled[:2].reshape(-1), here]).astype(jnp.int32)


def near(table, line, k):
    return table[NEAR + LINE * line + k]


def cluster_at(table, k):
    if k >= 0:
        return jnp.where(table[PLACE] + k < LINE, near(table, 1, k), near(table, 2, k))
    return jnp.where(table[PLACE] + k >= 0, near(table, 1, k + LINE), near(table, 0, k + LINE))


def hidden_kernel(group, table, *refs):
    many = len(group)
    xs, weights = refs[: 4 * many], refs[4 * many : 4 * many + 4]
    outs, (gate_sum, up_sum) = refs[4 * many + 4 : 5 * many + 4], refs[5 * many + 4 :]
    step = pl.program_id(0)
    mine = near(table, 1, 0)

    @pl.when(step == 0)
    def _():
        gate_sum[...] = jnp.zeros_like(gate_sum)
        up_sum[...] = jnp.zeros_like(up_sum)

    for side in range(2):
        rows = []
        for n, k in enumerate(group):
            ahead, behind = xs[4 * n + side], xs[4 * n + 2 + side]
            rows.append(ahead[...] if k == 0 else jnp.where(cluster_at(table, k) == mine, ahead[...], behind[...]))
        rows = jnp.concatenate(rows, axis=0)
        gate_sum[...] += jnp.dot(rows, weights[side][...], preferred_element_type=jnp.float32)
        up_sum[...] += jnp.dot(rows, weights[2 + side][...], preferred_element_type=jnp.float32)

    @pl.when(step == pl.num_programs(0) - 1)
    def _():
        gate = gate_sum[...]
        value = gate / (1.0 + jnp.exp(-gate)) * up_sum[...]
        part = outs[0].shape[0]
        for n, k in enumerate(group):
            block = value[n * part : (n + 1) * part].astype(jnp.bfloat16)
            inside = (cluster_at(table, k) == mine) | (cluster_at(table, k - LINE if k else 0) == mine)
            outs[n][...] = jnp.where(inside, block, jnp.zeros_like(block))


def hidden_of(table, group, ahead, behind, weights):
    part, width = ahead[0].shape
    half, units = weights[0].shape
    steps = half // TILE
    own_half = pl.BlockSpec((part, TILE), lambda i, t: (0, t[CORE] * steps + i))
    other_half = pl.BlockSpec((part, TILE), lambda i, t: (0, (1 - t[CORE]) * steps + i))
    weight = pl.BlockSpec((TILE, units), lambda i, t: (i, 0))
    args, specs = [], []
    for k in group:
        args += [ahead[k], ahead[k], behind[k], behind[k]]
        specs += [own_half, other_half, own_half, other_half]
    rows = part * len(group)
    return pl.pallas_call(
        functools.partial(hidden_kernel, group),
        out_shape=[jax.ShapeDtypeStruct((part, units), jnp.bfloat16)] * len(group),
        grid_spec=pltpu.PrefetchScalarGridSpec(
            num_scalar_prefetch=1,
            grid=(steps,),
            in_specs=specs + [weight] * 4,
            out_specs=[pl.BlockSpec((part, units), lambda i, t: (0, 0))] * len(group),
            scratch_shapes=[pltpu.VMEM((rows, units), jnp.float32)] * 2,
        ),
        compiler_params=pltpu.CompilerParams(vmem_limit_bytes=40 << 20),
        cost_estimate=pl.CostEstimate(
            flops=4 * rows * width * units, bytes_accessed=8 * half * units + 4 * rows * width, transcendentals=rows * units
        ),
        name="hidden",
    )(table, *args, *weights)


def goes_on(table, to):
    edge = (LINE - 1 - table[PLACE]) if to == 0 else (LINE - table[PLACE]) % LINE
    return near(table, to, edge) == near(table, 1, 0)


def dom_of(table, line):
    return table[DOM + LINE * line]


def share_kernel(table, *refs):
    returned, outs = refs[:LINE], refs[LINE:]
    own = dom_of(table, 1)
    targets = (own, jnp.where(goes_on(table, 2), own, dom_of(table, 2)), jnp.where(goes_on(table, 0), own, dom_of(table, 0)))
    for out, target in zip(outs, targets):
        place = (target - table[PLACE]) & (LINE - 1)
        for k in range(LINE):

            @pl.when(place == k)
            def _():
                out[...] = returned[k][...]


def send_kernel(table, own, nxt, last, came_last, came_next, *outs):
    line = table[LINE_AT]
    dom = [lax.div(dom_of(table, n) + LINE, LINE) - 1 for n in range(3)]
    at_own = jnp.where(dom[1] == line, 0, jnp.where(dom[1] > line, 4, 3))
    at_last = jnp.where(dom[0] == line, 2, 3)
    at_next = jnp.where(dom[2] == line, 1, 4)
    sources = (own, nxt, last, came_last, came_next)
    for away in range(LINE):
        wanted = near(table, 1, away)
        source = jnp.where(wanted == near(table, 0, 0), at_last, jnp.where(wanted == near(table, 2, 0), at_next, at_own))
        for n, ref in enumerate(sources):

            @pl.when(source == n)
            def _():
                outs[away][...] = ref[...]


def forward_kernel(table, back_three, ahead_six, ahead_three, back_six, to_next, to_last):
    def pick(out, far, near_by, receiver):
        wants_far = cluster_at(table, 6 * receiver) == cluster_at(table, receiver)

        @pl.when(wants_far)
        def _():
            out[...] = far[...]

        @pl.when(jnp.logical_not(wants_far))
        def _():
            out[...] = near_by[...]

    pick(to_next, ahead_six, back_three, 1)
    pick(to_last, back_six, ahead_three, -1)


def choose(kernel, table, arrays, outs, name):
    whole = pl.BlockSpec(memory_space=pltpu.VMEM)
    shape = jax.ShapeDtypeStruct(arrays[0].shape, arrays[0].dtype)
    size = 2 * arrays[0].size
    return pl.pallas_call(
        kernel,
        out_shape=[shape] * outs,
        in_specs=[pl.BlockSpec(memory_space=pltpu.SMEM)] + [whole] * len(arrays),
        out_specs=[whole] * outs,
        compiler_params=pltpu.CompilerParams(vmem_limit_bytes=24 << 20),
        cost_estimate=pl.CostEstimate(flops=0, bytes_accessed=size * (len(arrays) + outs), transcendentals=0),
        name=name,
    )(table, *arrays)


def correlate_kernel(add, table, *refs):
    hidden, panel = refs[:LINE], refs[LINE : 2 * LINE]
    out = refs[-1]
    left = jnp.concatenate([ref[...] for ref in hidden], axis=0)
    right = jnp.concatenate([ref[...] for ref in panel], axis=0)
    sums = lax.dot_general(left, right, (((0,), (0,)), ((), ())), preferred_element_type=jnp.float32)
    if add:
        rows = jnp.full((1, 1), table[SIZE] * ROWS, jnp.int32).astype(jnp.float32)
        sums = (sums + refs[2 * LINE][...]) / jnp.sqrt(rows)
    out[...] = sums


def correlate(table, hidden, panel, received=None):
    part, units = hidden[0].shape
    add = received is not None
    core = (lambda t: t[CORE]) if add else (lambda t: 1 - t[CORE])
    tile = 128
    steps = units // 2 // tile
    left = pl.BlockSpec((part, tile), lambda i, t: (0, core(t) * steps + i))
    right = pl.BlockSpec((part, units), lambda i, t: (0, 0))
    result = pl.BlockSpec((tile, units), lambda i, t: (i, 0))
    extra = [received] if add else []
    return pl.pallas_call(
        functools.partial(correlate_kernel, add),
        out_shape=jax.ShapeDtypeStruct((units // 2, units), jnp.float32),
        grid_spec=pltpu.PrefetchScalarGridSpec(
            num_scalar_prefetch=1,
            grid=(steps,),
            in_specs=[left] * LINE + [right] * LINE + [result] * len(extra),
            out_specs=result,
        ),
        compiler_params=pltpu.CompilerParams(vmem_limit_bytes=24 << 20),
        cost_estimate=pl.CostEstimate(
            flops=LINE * part * units * units, bytes_accessed=32 * part * units, transcendentals=0
        ),
        name="correlate",
    )(table, *hidden, *panel, *extra)


def per_device(calib_rows, gate_weight, up_weight, cluster, dominant_rank):
    table = scalars(cluster, dominant_rank)

    gate, up = gate_weight[0], up_weight[0]
    gate_other, up_other = swap_cores(gate), swap_cores(up)
    own = calib_rows[0]
    ahead, behind = {0: own}, {0: own}
    ahead[1], behind[7] = with_next(own), with_last(own)
    ahead[1], behind[7], gate_other, up_other = after(ahead[1], behind[7], gate_other, up_other)
    weights = (gate, gate_other, up, up_other)
    behind[6], ahead[2] = with_last(ahead[1]), with_next(behind[7])
    behind[1], ahead[7] = to_line(ahead[1], 1), to_line(behind[7], -1)
    ahead[2], behind[6], behind[1], ahead[7] = after(ahead[2], behind[6], behind[1], ahead[7])
    behind[5], ahead[3] = with_last(ahead[2]), with_next(behind[6])
    behind[2], ahead[6] = to_line(ahead[2], 1), to_line(behind[6], -1)

    hidden, returned = {}, {}

    def compute(group):
        for k, block in zip(group, hidden_of(table, group, ahead, behind, weights)):
            hidden[k] = block
            if k:
                block, seen_at = round_line(block, k)
                returned[seen_at] = block

    compute((0, 1, 7))
    own_hidden = hidden[0]
    ahead[3], behind[5], ahead[6], behind[2], own_hidden = after(ahead[3], behind[5], ahead[6], behind[2], own_hidden)
    to_next, to_last = choose(forward_kernel, table, [behind[5], ahead[6], ahead[3], behind[2]], 2, "forward")
    from_next, from_last = with_next(to_next), with_last(to_last)
    ahead[4], behind[3], behind[4], ahead[5] = from_next, from_next, from_last, from_last
    compute((2, 6))
    compute((3, 5, 4))
    hidden[0] = returned[0] = own_hidden

    shares = choose(share_kernel, table, [returned[k] for k in range(LINE)], 3, "share")
    came_last, came_next = to_line(shares[1], 1), to_line(shares[2], -1)
    chunks = choose(send_kernel, table, [*shares, came_last, came_next], LINE, "send")
    panel = {0: chunks[0]}
    for away in range(1, LINE):
        block, seen_at = round_line(chunks[away], away)
        panel[seen_at] = block

    hidden, panel = [hidden[k] for k in range(LINE)], [panel[k] for k in range(LINE)]
    received = swap_cores(correlate(table, hidden, panel))
    return correlate(table, hidden, panel, received)[None]


def solution(mesh):
    return jax.shard_map(
        per_device,
        mesh=mesh,
        in_specs=(
            P("expert", "row", None),
            P("expert", "row", None),
            P("expert", "row", None),
            P(),
            P(),
        ),
        out_specs=P("expert", "row", None),
        check_vma=False,
    )
```

```python
import functools

import jax
import jax.numpy as jnp
from jax import lax
from jax.experimental import pallas as pl
from jax.experimental.pallas import tpu as pltpu
from jax.sharding import PartitionSpec as P

ROWS = 128
LINE = 8
TILE = 512

NEAR, DOM, CORE, LINE_AT, PLACE, SIZE = 0, 24, 48, 49, 50, 51


def moved(value, target):
    count = lax.axis_size("expert")
    return lax.ppermute(value, "expert", [(i, target(i, count)) for i in range(count)])


def with_next(value):
    return moved(value, lambda i, count: i + 1 - 2 * (i % 2))


def with_last(value, cyclic=True):
    def target(i, count):
        other = i - 1 + 2 * (i % 2)
        return other if 0 <= other < count else other % count if cyclic else i

    return moved(value, target)


def to_line(value, step, cyclic=True):
    def target(i, count):
        turn = 1 - 2 * (i % 2)
        other = i + step * LINE * turn
        return other if 0 <= other < count else other % count if cyclic else i + turn

    return moved(value, target)


def round_line(value, offset):
    turn = lambda i, count: i // LINE * LINE + (i + offset * (1 - 2 * (i % 2))) % LINE
    return moved(value, turn), (offset if offset % 2 else LINE - offset)


def swap_cores(value):
    return lax.ppermute(value, "row", [(0, 1), (1, 0)])


def after(*values):
    return lax.optimization_barrier(values)


def scalars(cluster, dominant_rank):
    expert_id = lax.axis_index("expert")
    top = cluster.shape[0] - 1
    mirrored = expert_id % 2 == 1
    expert_id = jnp.where(mirrored, top - expert_id, expert_id)
    line, place = expert_id // LINE, expert_id % LINE
    start = jnp.sum((cluster[None, :] < cluster[:, None]).astype(jnp.int32), axis=1)
    size = jnp.sum((cluster[None, :] == cluster[:, None]).astype(jnp.int32), axis=1)
    names = jnp.arange(dominant_rank.shape[0], dtype=jnp.int32)
    rank = jnp.sum(jnp.where(names[None, :] == cluster[:, None], dominant_rank[None, :], 0), axis=1)
    dom = start + rank % size
    tables = jnp.where(mirrored, jnp.stack([cluster, top - dom, size])[:, ::-1], jnp.stack([cluster, dom, size]))
    tables = jnp.pad(tables, ((0, 0), (LINE, LINE)), constant_values=-1)
    three = lax.dynamic_slice_in_dim(tables, line * LINE, 3 * LINE, 1).reshape(3, 3, LINE)
    rolled = lax.dynamic_slice_in_dim(jnp.concatenate([three, three], axis=2), place, LINE, 2)
    here = jnp.stack([lax.axis_index("row"), line, place, rolled[2, 1, 0]])
    return jnp.concatenate([rolled[:2].reshape(-1), here]).astype(jnp.int32)


def near(table, line, k):
    return table[NEAR + LINE * line + k]


def cluster_at(table, k):
    if k >= 0:
        return jnp.where(table[PLACE] + k < LINE, near(table, 1, k), near(table, 2, k))
    return jnp.where(table[PLACE] + k >= 0, near(table, 1, k + LINE), near(table, 0, k + LINE))


def hidden_kernel(group, table, *refs):
    many = len(group)
    xs, weights = refs[: 4 * many], refs[4 * many : 4 * many + 4]
    outs, (gate_sum, up_sum) = refs[4 * many + 4 : 5 * many + 4], refs[5 * many + 4 :]
    step = pl.program_id(0)
    mine = near(table, 1, 0)

    @pl.when(step == 0)
    def _():
        gate_sum[...] = jnp.zeros_like(gate_sum)
        up_sum[...] = jnp.zeros_like(up_sum)

    for side in range(2):
        rows = []
        for n, k in enumerate(group):
            ahead, behind = xs[4 * n + side], xs[4 * n + 2 + side]
            rows.append(ahead[...] if k == 0 else jnp.where(cluster_at(table, k) == mine, ahead[...], behind[...]))
        rows = jnp.concatenate(rows, axis=0)
        gate_sum[...] += jnp.dot(rows, weights[side][...], preferred_element_type=jnp.float32)
        up_sum[...] += jnp.dot(rows, weights[2 + side][...], preferred_element_type=jnp.float32)

    @pl.when(step == pl.num_programs(0) - 1)
    def _():
        gate = gate_sum[...]
        value = gate / (1.0 + jnp.exp(-gate)) * up_sum[...]
        part = outs[0].shape[0]
        for n, k in enumerate(group):
            block = value[n * part : (n + 1) * part].astype(jnp.bfloat16)
            inside = (cluster_at(table, k) == mine) | (cluster_at(table, k - LINE if k else 0) == mine)
            outs[n][...] = jnp.where(inside, block, jnp.zeros_like(block))


def hidden_of(table, group, ahead, behind, weights):
    part, width = ahead[0].shape
    half, units = weights[0].shape
    steps = half // TILE
    own_half = pl.BlockSpec((part, TILE), lambda i, t: (0, t[CORE] * steps + i))
    other_half = pl.BlockSpec((part, TILE), lambda i, t: (0, (1 - t[CORE]) * steps + i))
    weight = pl.BlockSpec((TILE, units), lambda i, t: (i, 0))
    args, specs = [], []
    for k in group:
        args += [ahead[k], ahead[k], behind[k], behind[k]]
        specs += [own_half, other_half, own_half, other_half]
    rows = part * len(group)
    return pl.pallas_call(
        functools.partial(hidden_kernel, group),
        out_shape=[jax.ShapeDtypeStruct((part, units), jnp.bfloat16)] * len(group),
        grid_spec=pltpu.PrefetchScalarGridSpec(
            num_scalar_prefetch=1,
            grid=(steps,),
            in_specs=specs + [weight] * 4,
            out_specs=[pl.BlockSpec((part, units), lambda i, t: (0, 0))] * len(group),
            scratch_shapes=[pltpu.VMEM((rows, units), jnp.float32)] * 2,
        ),
        compiler_params=pltpu.CompilerParams(vmem_limit_bytes=40 << 20),
        cost_estimate=pl.CostEstimate(
            flops=4 * rows * width * units, bytes_accessed=8 * half * units + 4 * rows * width, transcendentals=rows * units
        ),
        name="hidden",
    )(table, *args, *weights)


def goes_on(table, to):
    edge = (LINE - 1 - table[PLACE]) if to == 0 else (LINE - table[PLACE]) % LINE
    return near(table, to, edge) == near(table, 1, 0)


def dom_of(table, line):
    return table[DOM + LINE * line]


def share_kernel(table, *refs):
    returned, outs = refs[:LINE], refs[LINE:]
    own = dom_of(table, 1)
    targets = (own, jnp.where(goes_on(table, 2), own, dom_of(table, 2)), jnp.where(goes_on(table, 0), own, dom_of(table, 0)))
    for out, target in zip(outs, targets):
        place = (target - table[PLACE]) & (LINE - 1)
        for k in range(LINE):

            @pl.when(place == k)
            def _():
                out[...] = returned[k][...]


def send_kernel(table, own, nxt, last, came_last, came_next, *outs):
    line = table[LINE_AT]
    dom = [lax.div(dom_of(table, n) + LINE, LINE) - 1 for n in range(3)]
    at_own = jnp.where(dom[1] == line, 0, jnp.where(dom[1] > line, 4, 3))
    at_last = jnp.where(dom[0] == line, 2, 3)
    at_next = jnp.where(dom[2] == line, 1, 4)
    sources = (own, nxt, last, came_last, came_next)
    for away in range(LINE):
        wanted = near(table, 1, away)
        source = jnp.where(wanted == near(table, 0, 0), at_last, jnp.where(wanted == near(table, 2, 0), at_next, at_own))
        for n, ref in enumerate(sources):

            @pl.when(source == n)
            def _():
                outs[away][...] = ref[...]


def forward_kernel(table, back_three, ahead_six, ahead_three, back_six, to_next, to_last):
    def pick(out, far, near_by, receiver):
        wants_far = cluster_at(table, 6 * receiver) == cluster_at(table, receiver)

        @pl.when(wants_far)
        def _():
            out[...] = far[...]

        @pl.when(jnp.logical_not(wants_far))
        def _():
            out[...] = near_by[...]

    pick(to_next, ahead_six, back_three, 1)
    pick(to_last, back_six, ahead_three, -1)


def choose(kernel, table, arrays, outs, name):
    whole = pl.BlockSpec(memory_space=pltpu.VMEM)
    shape = jax.ShapeDtypeStruct(arrays[0].shape, arrays[0].dtype)
    size = 2 * arrays[0].size
    return pl.pallas_call(
        kernel,
        out_shape=[shape] * outs,
        in_specs=[pl.BlockSpec(memory_space=pltpu.SMEM)] + [whole] * len(arrays),
        out_specs=[whole] * outs,
        compiler_params=pltpu.CompilerParams(vmem_limit_bytes=24 << 20),
        cost_estimate=pl.CostEstimate(flops=0, bytes_accessed=size * (len(arrays) + outs), transcendentals=0),
        name=name,
    )(table, *arrays)


def correlate_kernel(add, table, *refs):
    hidden, panel = refs[:LINE], refs[LINE : 2 * LINE]
    out = refs[-1]
    left = jnp.concatenate([ref[...] for ref in hidden], axis=0)
    right = jnp.concatenate([ref[...] for ref in panel], axis=0)
    sums = lax.dot_general(left, right, (((0,), (0,)), ((), ())), preferred_element_type=jnp.float32)
    if add:
        rows = jnp.full((1, 1), table[SIZE] * ROWS, jnp.int32).astype(jnp.float32)
        sums = (sums + refs[2 * LINE][...]) / jnp.sqrt(rows)
    out[...] = sums


def correlate(table, hidden, panel, received=None):
    part, units = hidden[0].shape
    add = received is not None
    core = (lambda t: t[CORE]) if add else (lambda t: 1 - t[CORE])
    tile = 128
    steps = units // 2 // tile
    left = pl.BlockSpec((part, tile), lambda i, t: (0, core(t) * steps + i))
    right = pl.BlockSpec((part, units), lambda i, t: (0, 0))
    result = pl.BlockSpec((tile, units), lambda i, t: (i, 0))
    extra = [received] if add else []
    return pl.pallas_call(
        functools.partial(correlate_kernel, add),
        out_shape=jax.ShapeDtypeStruct((units // 2, units), jnp.float32),
        grid_spec=pltpu.PrefetchScalarGridSpec(
            num_scalar_prefetch=1,
            grid=(steps,),
            in_specs=[left] * LINE + [right] * LINE + [result] * len(extra),
            out_specs=result,
        ),
        compiler_params=pltpu.CompilerParams(vmem_limit_bytes=24 << 20),
        cost_estimate=pl.CostEstimate(
            flops=LINE * part * units * units, bytes_accessed=32 * part * units, transcendentals=0
        ),
        name="correlate",
    )(table, *hidden, *panel, *extra)


def per_device(calib_rows, gate_weight, up_weight, cluster, dominant_rank):
    table = scalars(cluster, dominant_rank)

    gate, up = gate_weight[0], up_weight[0]
    gate_other, up_other = swap_cores(gate), swap_cores(up)
    own = calib_rows[0]
    ahead, behind = {0: own}, {0: own}
    ahead[1], behind[7] = with_next(own), with_last(own)
    ahead[1], behind[7], gate_other, up_other = after(ahead[1], behind[7], gate_other, up_other)
    weights = (gate, gate_other, up, up_other)
    behind[6], ahead[2] = with_last(ahead[1]), with_next(behind[7])
    behind[1], ahead[7] = to_line(ahead[1], 1), to_line(behind[7], -1)
    ahead[2], behind[6], behind[1], ahead[7] = after(ahead[2], behind[6], behind[1], ahead[7])
    behind[5], ahead[3] = with_last(ahead[2], cyclic=False), with_next(behind[6])
    behind[2], ahead[6] = to_line(ahead[2], 1), to_line(behind[6], -1)

    hidden, returned = {}, {}

    def compute(group):
        for k, block in zip(group, hidden_of(table, group, ahead, behind, weights)):
            hidden[k] = block
            if k:
                block, seen_at = round_line(block, k)
                returned[seen_at] = block

    compute((0, 1, 7))
    own_hidden = hidden[0]
    ahead[3], behind[5], ahead[6], behind[2], own_hidden = after(ahead[3], behind[5], ahead[6], behind[2], own_hidden)
    to_next, to_last = choose(forward_kernel, table, [behind[5], ahead[6], ahead[3], behind[2]], 2, "forward")
    from_next, from_last = with_next(to_next), with_last(to_last)
    ahead[4], behind[3], behind[4], ahead[5] = from_next, from_next, from_last, from_last
    compute((2, 6))
    compute((3, 5, 4))
    hidden[0] = returned[0] = own_hidden

    shares = choose(share_kernel, table, [returned[k] for k in range(LINE)], 3, "share")
    came_last, came_next = to_line(shares[1], 1, cyclic=False), to_line(shares[2], -1, cyclic=False)
    chunks = choose(send_kernel, table, [*shares, came_last, came_next], LINE, "send")
    panel = {0: chunks[0]}
    for away in range(1, LINE):
        block, seen_at = round_line(chunks[away], away)
        panel[seen_at] = block

    hidden, panel = [hidden[k] for k in range(LINE)], [panel[k] for k in range(LINE)]
    received = swap_cores(correlate(table, hidden, panel))
    return correlate(table, hidden, panel, received)[None]


def solution(mesh):
    return jax.shard_map(
        per_device,
        mesh=mesh,
        in_specs=(
            P("expert", "row", None),
            P("expert", "row", None),
            P("expert", "row", None),
            P(),
            P(),
        ),
        out_specs=P("expert", "row", None),
        check_vma=False,
    )
```
